32 devices in a mesh: sub: 8 (over z, y), coarse: 4 (over x, core).
Axes of the slice: x: 2, y: 2, z: 4, core: 2. Of those that a mesh axis runs over, the one named last changes fastest.
Arguments:
- right_side: float32 [8, 24576], P(None, 'sub'), may hold values from -6 to 6
- dual_ops: bfloat16 [32, 1536, 1536], P('sub', 'coarse'), may hold values from -8 to 72, as said below
- precond_ops: bfloat16 [32, 1536, 1536], P('sub', 'coarse'), may hold values from -8 to 72, as said below
- corner_ops: bfloat16 [32, 24, 1536], P('sub'), may hold values from -0.15625 to 0.15625
- coarse_inverse: float32 [64, 64], P('coarse'), may hold values from -8 to 72, as said below
- sub_index: int32 [32, 1536], P('sub'), may hold values from 0 to 24575, as said below
- corner_map: int32 [32, 24], P('sub'), may hold values from 0 to 63
Outputs:
- multipliers: float32 [8, 24576], P(None, 'sub')
- residual: float32 [8, 24576], P(None, 'sub')
The draws below stay inside these ranges and needn't reach their ends.
Inputs may be any that keep to these rules, and one draw needn't show every extreme that they name: `sub_index`: every multiplier number stands in exactly two slots in all: one in the first half of some subdomain's slots and one in the second half of some subdomain's slots. With multiplier i owned by index i // 3072 of sub and subdomain s by index s // 4, a subdomain's first-half slots hold only multipliers of its own index, its second-half slots only multipliers of its own index or of the index before it (cyclically), and half of every index's multipliers have their second slot on the next index. `dual_ops`: symmetric positive definite. `precond_ops`: symmetric positive definite. `coarse_inverse`: symmetric positive definite.
All inputs are finite; a program needn't handle non-finite values.
Results may differ from the reference program's by a relative error of at most 0.022.
Values may be sent and summed in bfloat16 or wider, within the bound.
A program may use at most 128 MiB of HBM per device.

```python
import math
import jax
import jax.numpy as jnp
from jax import lax

M_LOC = 1536
SUB_DEV = 4
CASES = 8
NC = 24
ITERS = 4
NSUBS = 32
LAM_DEV = 3072
NLAM = 24576
NCG = 64


def dominant(key, count, order):
    first, second = jax.random.split(key, 2)
    off = jax.random.uniform(first, (count, order, order), jnp.float32, -1.0, 1.0) * (2.4 / math.sqrt(order))
    off = 0.5 * (off + jnp.swapaxes(off, 1, 2))
    eye = jnp.eye(order, dtype=jnp.float32)
    diag = jax.random.uniform(second, (count, order, 1), jnp.float32, 2.5, 4.5)
    return off * (1.0 - eye) + eye * diag


def draw_dual_ops(key, part):
    key = jax.random.fold_in(key, 1)
    mats = dominant(key, NSUBS, M_LOC)
    return mats.astype(jnp.bfloat16)


def draw_precond_ops(key, part):
    key = jax.random.fold_in(key, 2)
    mats = dominant(key, NSUBS, M_LOC)
    return mats.astype(jnp.bfloat16)


def draw_coarse_inverse(key, part):
    key = jax.random.fold_in(key, 3)
    mats = dominant(key, 1, NCG)
    return mats[0]


def draw_sub_index(key, part):
    key = jax.random.fold_in(key, 4)
    owners = NSUBS // SUB_DEV
    first_key, second_key, third_key = jax.random.split(key, 3)
    first = jax.vmap(lambda k: jax.random.permutation(k, LAM_DEV))(jax.random.split(first_key, owners))
    chosen = jax.vmap(lambda k: jax.random.permutation(k, LAM_DEV))(jax.random.split(second_key, owners))
    order = jax.vmap(lambda k: jax.random.permutation(k, LAM_DEV))(jax.random.split(third_key, owners))
    base = jnp.arange(owners, dtype=jnp.int32)[:, None] * LAM_DEV
    first_glob = base + first.astype(jnp.int32)
    kept = base + chosen[:, LAM_DEV // 2:].astype(jnp.int32)
    sent = base + chosen[:, :LAM_DEV // 2].astype(jnp.int32)
    pool = jnp.concatenate([kept, jnp.roll(sent, 1, axis=0)], axis=1)
    second = jnp.take_along_axis(pool, order.astype(jnp.int32), axis=1)
    half = M_LOC // 2
    first_glob = first_glob.reshape(owners, SUB_DEV, half)
    second = second.reshape(owners, SUB_DEV, half)
    return jnp.concatenate([first_glob, second], axis=2).reshape(NSUBS, M_LOC).astype(jnp.int32)


def place_ends(drawn, rng, low, high):
    longest = drawn.shape.index(max(drawn.shape))
    spots = []
    for shift in (0, 1):
        where = [jax.random.randint(jax.random.fold_in(rng, axis), (), 0, length) for axis, length in enumerate(drawn.shape)]
        where[longest] = (where[longest] + shift) % drawn.shape[longest]
        spots.append(tuple(where))
    return drawn.at[spots[0]].set(low).at[spots[1]].set(high)


def shard_levels(own_key, extent, pieces, low, high):
    factor_of, own = 1.0, jax.random.fold_in(own_key, 6)
    for position, shards_of in pieces:
        draws = jnp.exp(jax.random.uniform(jax.random.fold_in(own, position), (shards_of,), jnp.float32, low / len(pieces), high / len(pieces)))
        factor_of = factor_of * jnp.repeat(draws, extent[position] // shards_of).reshape([-1 if axis == position else 1 for axis in range(len(extent))])
    return factor_of


def centred(rng, dims, spread, limit, cuts=(), kind=jnp.bfloat16):
    array = jax.random.normal(rng, dims, jnp.float32) * spread
    if len(cuts) > 0:
        array = shard_levels(rng, dims, cuts, -0.22, 0.18) * array
    return jnp.clip(array, min=-limit, max=limit).astype(kind)


def setup_inputs(seed: int = 0) -> dict:
    splits = jax.random.split(jax.random.key(seed), 8)
    right_side = centred(splits[0], (CASES, NLAM), 1.0, 6.0, ((1, 8),), jnp.float32)
    dual_ops = draw_dual_ops(jax.random.fold_in(splits[7], 71), 0)
    precond_ops = draw_precond_ops(jax.random.fold_in(splits[7], 71), 0)
    corner_ops = centred(splits[3], (NSUBS, NC, M_LOC), M_LOC ** -0.5, 0.15625, ((0, 8),))
    coarse_inverse = draw_coarse_inverse(jax.random.fold_in(splits[7], 71), 0)
    sub_index = draw_sub_index(jax.random.fold_in(splits[7], 71), 0)
    corner_map = place_ends(jax.random.randint(splits[6], (NSUBS, NC), 0, NCG), jax.random.fold_in(splits[6], 1), 0, NCG - 1).astype(jnp.int32)
    return dict(right_side=right_side, dual_ops=dual_ops, precond_ops=precond_ops, corner_ops=corner_ops, coarse_inverse=coarse_inverse, sub_index=sub_index, corner_map=corner_map)


HIGH = lax.Precision.HIGHEST


def apply_operator(vectors, matrices, corner_ops, coarse_inverse, sub_index, corner_map, with_coarse):
    order = matrices.shape[1]
    signs = jnp.where(jnp.arange(order) < order // 2, 1.0, -1.0).astype(jnp.float32)
    gathered = (vectors[:, sub_index] * signs).astype(jnp.bfloat16)

    def single(pair):
        return jnp.dot(pair[0], pair[1].T, preferred_element_type=jnp.float32)

    terms = lax.map(single, (matrices, jnp.transpose(gathered, (1, 0, 2))))
    terms = jnp.transpose(terms, (2, 0, 1))
    if with_coarse:
        corner_wide = corner_ops.astype(jnp.float32)
        lifted = jnp.einsum("scn,ksn->ksc", corner_wide, gathered.astype(jnp.float32), precision=HIGH)
        load = jnp.zeros((vectors.shape[0], coarse_inverse.shape[0]), jnp.float32).at[:, corner_map].add(lifted)
        answer = jnp.dot(load, coarse_inverse.T, precision=HIGH).astype(jnp.bfloat16)
        spread_back = answer[:, corner_map].astype(jnp.float32)
        terms = terms + jnp.einsum("scm,ksc->ksm", corner_wide, spread_back, precision=HIGH)
    return jnp.zeros(vectors.shape, jnp.float32).at[:, sub_index].add(terms * signs)


def reference(right_side, dual_ops, precond_ops, corner_ops, coarse_inverse, sub_index, corner_map):
    multipliers = jnp.zeros_like(right_side)
    residual = right_side
    pre = apply_operator(residual, precond_ops, corner_ops, coarse_inverse, sub_index, corner_map, False)
    fit = jnp.sum(residual * pre, axis=1)
    direction = pre
    for step in range(ITERS):
        image = apply_operator(direction, dual_ops, corner_ops, coarse_inverse, sub_index, corner_map, True)
        alpha = fit / jnp.sum(direction * image, axis=1)
        multipliers = multipliers + alpha[:, None] * direction
        residual = residual - alpha[:, None] * image
        if step + 1 < ITERS:
            pre = apply_operator(residual, precond_ops, corner_ops, coarse_inverse, sub_index, corner_map, False)
            fit_next = jnp.sum(residual * pre, axis=1)
            direction = pre + (fit_next / fit)[:, None] * direction
            fit = fit_next
    return multipliers, residual
```

```python
import functools

import jax
import jax.numpy as jnp
from jax import lax
from jax.experimental import pallas as pl
from jax.experimental.pallas import tpu as pltpu
from jax.sharding import PartitionSpec as P

ITERS = 4
LANES = 128
HIGH = lax.Precision.HIGHEST
MESH = pl.DeviceIdType.MESH
NT = (((1,), (1,)), ((), ()))


def passed_along(value, axis, steps):
    count = lax.axis_size(axis)
    pairs = [(source, (source + steps) % count) for source in range(count)]
    return lax.ppermute(value, axis, pairs)


def search(want_ref, col_ref, out_ref, width):
    group = 4 if (width // LANES) % 4 == 0 else 1
    span = group * LANES
    rows = col_ref.shape[0] // 8

    def outer(g, carry):
        want = [
            jnp.broadcast_to(
                want_ref[:, pl.ds(pl.multiple_of(g * span + i * LANES, LANES), LANES)], (8, LANES)
            )
            for i in range(group)
        ]

        def inner(k, accs):
            for u in range(8):
                row = k * 8 + u
                col = col_ref[pl.ds(pl.multiple_of(row * 8, 8), 8), :]
                accs = tuple(jnp.where(col == w, row, a) for w, a in zip(want, accs))
            return accs

        start = tuple(jnp.full((8, LANES), -1, jnp.int32) for _ in range(group))
        accs = lax.fori_loop(0, rows // 8, inner, start)
        sub = lax.broadcasted_iota(jnp.int32, (8, LANES), 0)
        for i in range(group):
            pos = jnp.max(accs[i] * 8 + sub, axis=0, keepdims=True)
            out_ref[:, pl.ds(pl.multiple_of(g * span + i * LANES, LANES), LANES)] = (
                jnp.broadcast_to(pos, (8, LANES))
            )
        return carry

    lax.fori_loop(0, width // span, outer, 0)


def search_kernel(first_ref, second_ref, own_ref, col_s_ref, col_f_ref, q1_ref, q2_ref, qo_ref):
    lam = own_ref.shape[1]
    search(first_ref, col_s_ref, q1_ref, lam)
    search(second_ref, col_f_ref, q2_ref, lam)
    search(own_ref, col_f_ref.at[pl.ds(0, lam)], qo_ref, lam)


def iterate_kernel(
    n_sub, rhs_ref, prev_ref, dual_ref, precond_ref, corner_ref, block_corner_ref, table_ref,
    kinv_ref, q1_ref, q2_ref, w1_ref, w2_ref, qo_ref,
    lam_out, res_out,
    D, R, L, V, S, rx, dtx, drx, ltx, lrx, ssem, rsem, dssem, drsem, lssem, lrsem,
):
    j = lax.axis_index("sub")
    c = lax.axis_index("coarse")
    subs, br, order = dual_ref.shape
    bw = subs * br
    half = 2 * bw
    hw = bw // 2
    right = lax.rem(j + 1, n_sub)
    left = lax.rem(j + n_sub - 1, n_sub)
    high = c // 2
    halo = lax.rem(j + 1 - 2 * high + n_sub, n_sub)
    halo_slot = 6 + c - 4 * high
    peers = [(j, lax.rem(c + o, 4)) for o in range(1, 4)]

    barrier = pltpu.get_barrier_semaphore()
    friends = list(peers)
    for o in range(4):
        friends += [(left, o), (right, o)]
    for o in range(2, n_sub - 1):
        friends.append((lax.rem(j + o, n_sub), c))
    for f in friends:
        pl.semaphore_signal(barrier, inc=1, device_id=f, device_id_type=MESH)
    pl.semaphore_wait(barrier, len(friends))

    def gather(idx_ref, src_ref, count, finish):
        def body(o, carry):
            at = pl.ds(pl.multiple_of(o * LANES, LANES), LANES)
            idx = idx_ref[:, at]
            lo = jnp.bitwise_and(idx, LANES - 1)
            hi = jnp.right_shift(idx, 7)
            acc = jnp.zeros((8, LANES), jnp.float32)
            for k in range(count):
                got = jnp.take_along_axis(
                    src_ref[:, k * LANES : (k + 1) * LANES], lo, axis=1,
                    mode="promise_in_bounds",
                )
                acc = jnp.where(hi == k, got, acc)
            finish(o, acc)
            return carry

        lax.fori_loop(0, half // LANES, body, 0)

    def put(ref, base, scale=None):
        def finish(o, acc):
            at = pl.ds(pl.multiple_of(base + o * LANES, LANES), LANES)
            ref[:, at] = acc

        return finish

    S[:, :half] = rhs_ref[...]
    S[:, half : 2 * half] = prev_ref[...]
    steps = half // LANES
    gather(w1_ref, S, 2 * steps, put(R, 0))
    gather(w2_ref, S, 2 * steps, put(R, half))
    D[...] = jnp.zeros_like(D)
    L[...] = jnp.zeros_like(L)

    def gathered(ref, s):
        parts = []
        for b in range(4):
            part = ref[:, b * bw + s * br : b * bw + (s + 1) * br]
            parts.append(part if b < 2 else -part)
        return jnp.concatenate(parts, axis=1).astype(jnp.bfloat16)

    def unpack(block):
        wide = block.astype(jnp.float32)
        return jnp.concatenate([wide[:8], wide[8:]], axis=1)

    def exchange(app, terms, vec_ref):
        rx[app, 0] = jnp.concatenate([terms[:, :hw], terms[:, hw:]], axis=0).astype(jnp.bfloat16)
        copies = []
        for i in range(7):
            if i < 3:
                slot, device = i + 1, peers[i]
            else:
                slot, device = halo_slot, (halo, i - 3)
            copy = pltpu.make_async_remote_copy(
                src_ref=rx.at[app, 0], dst_ref=rx.at[app, slot],
                send_sem=ssem.at[i], recv_sem=rsem.at[app, slot - 1],
                device_id=device, device_id_type=MESH,
            )
            copy.start()
            copies.append(copy)
        for slot in range(1, 8):
            pltpu.make_async_copy(
                rx.at[app, slot], rx.at[app, slot], rsem.at[app, slot - 1]
            ).wait()
        blocks = [unpack(rx[app, lax.rem(c + 4 - b, 4)]) for b in range(4)]
        part = jnp.zeros((8, LANES), jnp.float32)
        for b in range(4):
            prod = vec_ref[:, b * bw : (b + 1) * bw] * blocks[b]
            for k in range(bw // LANES):
                piece = prod[:, k * LANES : (k + 1) * LANES]
                part = part + piece if b < 2 else part - piece
        dtx[app] = part
        dots = []
        for o in range(1, n_sub):
            copy = pltpu.make_async_remote_copy(
                src_ref=dtx.at[app], dst_ref=drx.at[app, o - 1],
                send_sem=dssem.at[o - 1], recv_sem=drsem.at[app],
                device_id=(lax.rem(j + o, n_sub), c), device_id_type=MESH,
            )
            copy.start()
            dots.append(copy)
        V[:, :bw] = blocks[0]
        V[:, bw:half] = blocks[1]
        V[:, half : half + bw] = blocks[2]
        V[:, half + bw :] = blocks[3]
        S[:, :bw] = blocks[2]
        S[:, bw:half] = blocks[3]
        S[:, half : half + bw] = unpack(rx[app, 4])
        S[:, half + bw : 2 * half] = unpack(rx[app, 5])

        def less(o, acc):
            at = pl.ds(pl.multiple_of(o * LANES, LANES), LANES)
            S_first[:, at] = V[:, at]
            V[:, at] = V[:, at] - acc

        def more(o, acc):
            at = pl.ds(pl.multiple_of(half + o * LANES, LANES), LANES)
            V[:, at] = acc - V[:, at]

        S_first = S.at[:, pl.ds(2 * half, half)]
        gather(q1_ref, S, 2 * steps, less)
        S[:, :half] = S[:, 2 * half :]
        S[:, half : half + bw] = unpack(rx[app, 6])
        S[:, half + bw : 2 * half] = unpack(rx[app, 7])
        gather(q2_ref, S, 2 * steps, more)
        pltpu.make_async_copy(drx.at[app], drx.at[app], drsem.at[app]).wait()
        total = part
        for o in range(n_sub - 1):
            total = total + drx[app, o]
        for copy in copies + dots:
            copy.wait_send()
        return jnp.sum(total, axis=1, keepdims=True)

    def product(ops_ref, vecs):
        return [
            lax.dot_general(vecs[s], ops_ref[s], NT, preferred_element_type=jnp.float32)
            for s in range(subs)
        ]

    def body(step, fit):
        vecs = [gathered(R, s) for s in range(subs)]
        terms = jnp.concatenate(product(precond_ref, vecs), axis=1)
        fit_next = exchange(2 * step, terms, R)
        D[...] = V[...] + (fit_next / fit) * D[...]

        vecs = [gathered(D, s) for s in range(subs)]
        load = jnp.zeros((8, kinv_ref.shape[0]), jnp.float32)
        for s in range(subs):
            lifted = lax.dot_general(
                vecs[s], corner_ref[s], NT, preferred_element_type=jnp.float32
            )
            load = load + jnp.dot(
                lifted, table_ref[s], precision=HIGH, preferred_element_type=jnp.float32
            )
        ltx[step] = load
        loads = []
        for o in range(1, n_sub):
            copy = pltpu.make_async_remote_copy(
                src_ref=ltx.at[step], dst_ref=lrx.at[step, o - 1],
                send_sem=lssem.at[o - 1], recv_sem=lrsem.at[step],
                device_id=(lax.rem(j + o, n_sub), c), device_id_type=MESH,
            )
            copy.start()
            loads.append(copy)
        outs = product(dual_ref, vecs)
        pltpu.make_async_copy(lrx.at[step], lrx.at[step], lrsem.at[step]).wait()
        for o in range(n_sub - 1):
            load = load + lrx[step, o]
        answer = lax.dot_general(
            load, kinv_ref[...], NT, precision=HIGH, preferred_element_type=jnp.float32
        ).astype(jnp.bfloat16)
        wide = answer.astype(jnp.float32)
        for s in range(subs):
            spread = lax.dot_general(
                wide, table_ref[s], NT, preferred_element_type=jnp.float32
            ).astype(jnp.bfloat16)
            outs[s] = outs[s] + jnp.dot(
                spread, block_corner_ref[s], preferred_element_type=jnp.float32
            )
        energy = exchange(2 * step + 1, jnp.concatenate(outs, axis=1), D)
        for copy in loads:
            copy.wait_send()
        alpha = fit_next / energy
        L[...] = L[...] + alpha * D[:, :half]
        R[...] = R[...] - alpha * V[...]
        return fit_next

    lax.fori_loop(0, ITERS, body, jnp.ones((8, 1), jnp.float32))
    gather(qo_ref, L, steps, put(lam_out, 0))
    gather(qo_ref, R, steps, put(res_out, 0))


def per_device(
    right_side, dual_ops, precond_ops, corner_ops, coarse_inverse, sub_index, corner_map
):
    cases, lam = right_side.shape
    subs, br, order = dual_ops.shape
    ncg = coarse_inverse.shape[1]
    n_sub = lax.axis_size("sub")
    here = lax.axis_index("sub")
    mine = lax.axis_index("coarse")
    total = lam * n_sub
    slots = sub_index.reshape(subs, 4, br).transpose(1, 0, 2).reshape(-1)
    first, second = slots[:lam], slots[lam:]
    first_prev = passed_along(first, "sub", 1)
    second_next = passed_along(second, "sub", -1)
    prev = passed_along(right_side, "sub", 1)
    kinv = lax.all_gather(coarse_inverse, "coarse", axis=0, tiled=True)
    pad = -ncg % LANES
    kinv = jnp.pad(kinv, ((0, pad), (0, pad)))
    own = jnp.arange(lam, dtype=jnp.int32) + here * lam
    wide = lambda x: jnp.broadcast_to(x[:, None], (x.shape[0], LANES))
    col_s = wide(jnp.concatenate([second, second_next]))
    col_f = wide(jnp.concatenate([first, first_prev]))
    index = jax.ShapeDtypeStruct((8, lam), jnp.int32)
    vmem = pl.BlockSpec(memory_space=pltpu.VMEM)
    q1, q2, qo = pl.pallas_call(
        search_kernel,
        out_shape=[index] * 3,
        in_specs=[vmem] * 5,
        out_specs=[vmem] * 3,
        compiler_params=pltpu.CompilerParams(vmem_limit_bytes=32 * 2**20),
        name="search",
    )(first[None], second[None], own[None], col_s, col_f)
    spot = lambda x: jnp.broadcast_to(
        jnp.mod(x - here * lam + total, total)[None], (8, lam)
    )
    w1 = spot(first)
    w2 = spot(second)
    w2 = jnp.where(w2 < lam, w2, w2 - (total - lam) + lam)
    table = (corner_map[:, :, None] == jnp.arange(ncg + pad)[None, None, :]).astype(jnp.float32)
    block_corner = lax.dynamic_slice_in_dim(corner_ops, mine * br, br, 2)
    bw = subs * br
    f32 = lambda *dims: pltpu.VMEM(dims, jnp.float32)
    dma = pltpu.SemaphoreType.DMA
    out = jax.ShapeDtypeStruct((cases, lam), jnp.float32)
    return pl.pallas_call(
        functools.partial(iterate_kernel, n_sub),
        out_shape=[out, out],
        in_specs=[vmem] * 13,
        out_specs=[vmem] * 2,
        scratch_shapes=[
            f32(8, 2 * lam), f32(8, 2 * lam), f32(8, lam), f32(8, 2 * lam), f32(8, 3 * lam),
            pltpu.VMEM((2 * ITERS, 8, 16, bw // 2), jnp.bfloat16),
            f32(2 * ITERS, 8, LANES), f32(2 * ITERS, n_sub - 1, 8, LANES),
            f32(ITERS, 8, ncg + pad), f32(ITERS, n_sub - 1, 8, ncg + pad),
            dma((7,)), dma((2 * ITERS, 7)),
            dma((n_sub - 1,)), dma((2 * ITERS,)),
            dma((n_sub - 1,)), dma((ITERS,)),
        ],
        compiler_params=pltpu.CompilerParams(
            collective_id=0, has_side_effects=True, vmem_limit_bytes=40 * 2**20
        ),
        name="iterate",
    )(
        right_side, prev, dual_ops, precond_ops, corner_ops, block_corner, table,
        kinv, q1, q2, w1, w2, qo,
    )


def solution(mesh):
    placed = (
        P(None, "sub"),
        P("sub", "coarse", None),
        P("sub", "coarse", None),
        P("sub", None, None),
        P("coarse", None),
        P("sub", None),
        P("sub", None),
    )
    return jax.shard_map(
        per_device,
        mesh=mesh,
        in_specs=placed,
        out_specs=(P(None, "sub"), P(None, "sub")),
        check_vma=False,
    )
```

```python
import functools

import jax
import jax.numpy as jnp
from jax import lax
from jax.experimental import pallas as pl
from jax.experimental.pallas import tpu as pltpu
from jax.sharding import PartitionSpec as P

ITERS = 4
LANES = 128
WIDE = 256
SHIFT = 8
CHUNK = 512
HIGH = lax.Precision.HIGHEST
MESH = pl.DeviceIdType.MESH
NT = (((1,), (1,)), ((), ()))


def iterate_kernel(
    n_sub, rhs_ref, dual_hbm, precond_hbm, corner_ref, block_corner_ref, table_ref,
    part_ref, first_ref, second_ref,
    lam_out, res_out,
    dual_ref, precond_ref, D, R, L, V, prev_ref, first_prev, second_next, parts_ref, kinv_ref,
    Q1, Q2, QO, OH1, OH2, OHT,
    rx, dtx, drx, ltx, lrx, msem, psem, qsem, ssem, rsem, dssem, drsem, lssem, lrsem,
):
    j = lax.axis_index("sub")
    c = lax.axis_index("coarse")
    subs, br, order = dual_ref.shape
    bw = subs * br
    half = 2 * bw
    brows = bw // WIDE * 8
    kr = part_ref.shape[0]
    right = lax.rem(j + 1, n_sub)
    left = lax.rem(j + n_sub - 1, n_sub)
    high = c // 2
    halo = lax.rem(j + 1 - 2 * high + n_sub, n_sub)
    halo_slot = 6 + c - 4 * high
    peers = [(j, lax.rem(c + o, 4)) for o in range(1, 4)]

    loads = [
        pltpu.make_async_copy(precond_hbm, precond_ref, msem.at[0]),
        pltpu.make_async_copy(dual_hbm, dual_ref, msem.at[1]),
    ]
    for copy in loads:
        copy.start()

    barrier = pltpu.get_barrier_semaphore()
    friends = list(peers)
    for o in range(4):
        friends += [(left, o), (right, o)]
    for o in range(2, n_sub - 1):
        friends.append((lax.rem(j + o, n_sub), c))
    for f in friends:
        pl.semaphore_signal(barrier, inc=1, device_id=f, device_id_type=MESH)
    pl.semaphore_wait(barrier, len(friends))

    setup = []
    plan = [
        (first_ref, first_prev, (right, c)),
        (second_ref, second_next, (left, c)),
        (rhs_ref, prev_ref, (right, c)),
    ] + [(part_ref, parts_ref.at[o], peers[o]) for o in range(3)]
    for i, (source, target, device) in enumerate(plan):
        copy = pltpu.make_async_remote_copy(
            src_ref=source, dst_ref=target, send_sem=psem.at[i], recv_sem=qsem.at[i],
            device_id=device, device_id_type=MESH,
        )
        copy.start()
        setup.append(copy)

    step_w = CHUNK
    chunks = half // step_w

    def chunk_at(o):
        return pl.ds(pl.multiple_of(o * step_w, step_w), step_w)

    def build(oh_ref, idx_ref):
        def body(o, carry):
            low = jnp.bitwise_and(idx_ref[:1, chunk_at(o)], WIDE - 1)
            rows = lax.broadcasted_iota(jnp.int32, (WIDE, step_w), 0)
            oh_ref[:, chunk_at(o)] = jnp.where(rows == low, 1.0, 0.0).astype(jnp.bfloat16)
            return carry

        lax.fori_loop(0, chunks, body, 0)

    def gather(src, idx_ref, oh_ref, finish, parts=1):
        count = src.shape[0] // 8 // parts

        def body(o, carry):
            hi = jnp.right_shift(idx_ref[:, chunk_at(o)], SHIFT)
            hi = jnp.broadcast_to(hi, (8, step_w))
            got = jnp.dot(src, oh_ref[:, chunk_at(o)], preferred_element_type=jnp.float32)
            acc = jnp.zeros((8, step_w), jnp.float32)
            for h in range(count):
                val = got[h * 8 : h * 8 + 8]
                for p in range(1, parts):
                    at = (p * count + h) * 8
                    val = val + got[at : at + 8]
                acc = jnp.where(hi == h, val, acc)
            finish(o, acc)
            return carry

        lax.fori_loop(0, chunks, body, 0)

    def put(ref, base):
        def finish(o, acc):
            ref[:, pl.ds(pl.multiple_of(base + o * step_w, step_w), step_w)] = acc

        return finish

    def put_index(ref):
        def finish(o, acc):
            pos = (acc[0:1] * WIDE + acc[1:2]).astype(jnp.int32)
            ref[:, chunk_at(o)] = jnp.broadcast_to(pos, (8, step_w))

        return finish

    def to_rows(x):
        return jnp.concatenate(
            [x[:, i * WIDE : (i + 1) * WIDE] for i in range(x.shape[1] // WIDE)], axis=0
        )

    def split(x):
        x = to_rows(x)
        a = x.astype(jnp.bfloat16)
        x = x - a.astype(jnp.float32)
        b = x.astype(jnp.bfloat16)
        x = x - b.astype(jnp.float32)
        return jnp.concatenate([a, b, x.astype(jnp.bfloat16)], axis=0)

    def inverse(idx_ref, shift, base, total):
        nh = half // WIDE
        acc = jnp.zeros((nh * 8, WIDE), jnp.float32)
        for o in range(chunks):
            rel = idx_ref[:, o * step_w : (o + 1) * step_w] + shift
            rel = jnp.where(rel < 0, rel + total, rel)
            hi = jnp.right_shift(rel, SHIFT)
            low = jnp.bitwise_and(rel, WIDE - 1)
            pos = lax.broadcasted_iota(jnp.int32, (nh * 8, step_w), 1) + (base + o * step_w)
            row = lax.broadcasted_iota(jnp.int32, (nh * 8, step_w), 0)
            digit = jnp.bitwise_and(row, 7)
            val = jnp.where(digit == 0, jnp.right_shift(pos, SHIFT), jnp.bitwise_and(pos, WIDE - 1))
            keep = jnp.logical_and(jnp.right_shift(row, 3) == hi, digit < 2)
            left_side = jnp.where(keep, val, 0).astype(jnp.float32).astype(jnp.bfloat16)
            rows = lax.broadcasted_iota(jnp.int32, (WIDE, step_w), 0)
            right_side = jnp.where(rows == low, 1.0, 0.0).astype(jnp.bfloat16)
            acc = acc + lax.dot_general(
                left_side, right_side, NT, preferred_element_type=jnp.float32
            )
        return acc

    total = n_sub * half
    pf_own = inverse(first_ref, -j * half, 0, total)
    ps = inverse(second_ref, -j * half, 0, total)
    for h in range(half // WIDE):
        pos = (pf_own[h * 8 : h * 8 + 1] * WIDE + pf_own[h * 8 + 1 : h * 8 + 2]).astype(jnp.int32)
        QO[:, h * WIDE : (h + 1) * WIDE] = jnp.broadcast_to(pos, (8, WIDE))
    Q1[...] = jnp.broadcast_to(first_ref[...] - j * half, (8, half))
    rel = second_ref[...] - j * half
    rel = jnp.where(rel < 0, rel + total, rel)
    rel = jnp.where(rel < half, rel, rel - (total - 2 * half))
    Q2[...] = jnp.broadcast_to(rel, (8, half))
    build(OH1, Q1)
    build(OH2, Q2)
    D[...] = jnp.zeros_like(D)
    L[...] = jnp.zeros_like(L)
    kinv_ref[...] = jnp.zeros_like(kinv_ref)
    parts_ref[3] = part_ref[...]
    own_rows = split(rhs_ref[...])
    gather(own_rows, Q1, OH1, put(R, 0), 3)
    for copy in setup:
        copy.wait_recv()
    for b in range(4):
        kinv_ref[b * kr : (b + 1) * kr] = parts_ref[lax.rem(c + 7 - b, 4)]
    prev_rows = split(prev_ref[...])
    n = half // WIDE * 8
    both = []
    for p in range(3):
        both += [own_rows[p * n : (p + 1) * n], prev_rows[p * n : (p + 1) * n]]
    gather(jnp.concatenate(both, axis=0), Q2, OH2, put(R, half), 3)
    ps = ps + inverse(second_next, -j * half, half, total)
    pf_prev = inverse(first_prev, -left * half, half, total)
    gather(ps.astype(jnp.bfloat16), Q1, OH1, put_index(Q1))
    pf = jnp.concatenate([pf_own, pf_prev], axis=0).astype(jnp.bfloat16)
    gather(pf, Q2, OH2, put_index(Q2))
    build(OH1, Q1)
    build(OH2, Q2)
    for copy in setup:
        copy.wait_send()

    def gathered(ref, s):
        parts = []
        for b in range(4):
            part = ref[:, b * bw + s * br : b * bw + (s + 1) * br]
            parts.append(part if b < 2 else -part)
        return jnp.concatenate(parts, axis=1).astype(jnp.bfloat16)

    def unpack(block):
        wide = block.astype(jnp.float32)
        return jnp.concatenate([wide[i * 8 : i * 8 + 8] for i in range(brows // 8)], axis=1)

    def exchange(app, terms, vec_ref):
        rx[app, 0] = to_rows(terms).astype(jnp.bfloat16)
        copies = []
        for i in range(7):
            if i < 4:
                slot, device = halo_slot, (halo, i)
            else:
                slot, device = i - 3, peers[i - 4]
            copy = pltpu.make_async_remote_copy(
                src_ref=rx.at[app, 0], dst_ref=rx.at[app, slot],
                send_sem=ssem.at[i], recv_sem=rsem.at[app, slot - 1],
                device_id=device, device_id_type=MESH,
            )
            copy.start()
            copies.append(copy)
        for slot in range(1, 4):
            pltpu.make_async_copy(
                rx.at[app, slot], rx.at[app, slot], rsem.at[app, slot - 1]
            ).wait()
        packed = [rx[app, lax.rem(c + 4 - b, 4)] for b in range(4)]
        blocks = [unpack(p) for p in packed]
        part = jnp.zeros((8, LANES), jnp.float32)
        for b in range(4):
            prod = vec_ref[:, b * bw : (b + 1) * bw] * blocks[b]
            for k in range(bw // LANES):
                piece = prod[:, k * LANES : (k + 1) * LANES]
                part = part + piece if b < 2 else part - piece
        dtx[app] = part
        dots = []
        for o in range(1, n_sub):
            copy = pltpu.make_async_remote_copy(
                src_ref=dtx.at[app], dst_ref=drx.at[app, o - 1],
                send_sem=dssem.at[o - 1], recv_sem=drsem.at[app],
                device_id=(lax.rem(j + o, n_sub), c), device_id_type=MESH,
            )
            copy.start()
            dots.append(copy)
        for b in range(4):
            V[:, b * bw : (b + 1) * bw] = blocks[b]
        for slot in range(4, 8):
            pltpu.make_async_copy(
                rx.at[app, slot], rx.at[app, slot], rsem.at[app, slot - 1]
            ).wait()

        def less(o, acc):
            V[:, chunk_at(o)] = V[:, chunk_at(o)] - acc

        def more(o, acc):
            at = pl.ds(pl.multiple_of(half + o * step_w, step_w), step_w)
            V[:, at] = acc - V[:, at]

        gather(
            jnp.concatenate([packed[2], packed[3], rx[app, 4], rx[app, 5]], axis=0),
            Q1, OH1, less,
        )
        gather(
            jnp.concatenate([packed[0], packed[1], rx[app, 6], rx[app, 7]], axis=0),
            Q2, OH2, more,
        )
        pltpu.make_async_copy(drx.at[app], drx.at[app], drsem.at[app]).wait()
        total = part
        for o in range(n_sub - 1):
            total = total + drx[app, o]
        for copy in copies + dots:
            copy.wait_send()
        return jnp.sum(total, axis=1, keepdims=True)

    def product(ops_ref, vecs):
        return [
            lax.dot_general(vecs[s], ops_ref[s], NT, preferred_element_type=jnp.float32)
            for s in range(subs)
        ]

    for copy in loads:
        copy.wait()

    def body(step, fit):
        vecs = [gathered(R, s) for s in range(subs)]
        terms = jnp.concatenate(product(precond_ref, vecs), axis=1)
        fit_next = exchange(2 * step, terms, R)
        D[...] = V[...] + (fit_next / fit) * D[...]

        vecs = [gathered(D, s) for s in range(subs)]
        load = jnp.zeros((8, kinv_ref.shape[0]), jnp.float32)
        for s in range(subs):
            lifted = lax.dot_general(
                vecs[s], corner_ref[s], NT, preferred_element_type=jnp.float32
            )
            load = load + jnp.dot(
                lifted, table_ref[s], precision=HIGH, preferred_element_type=jnp.float32
            )
        ltx[step] = load
        sent = []
        for o in range(1, n_sub):
            copy = pltpu.make_async_remote_copy(
                src_ref=ltx.at[step], dst_ref=lrx.at[step, o - 1],
                send_sem=lssem.at[o - 1], recv_sem=lrsem.at[step],
                device_id=(lax.rem(j + o, n_sub), c), device_id_type=MESH,
            )
            copy.start()
            sent.append(copy)
        outs = product(dual_ref, vecs)
        pltpu.make_async_copy(lrx.at[step], lrx.at[step], lrsem.at[step]).wait()
        for o in range(n_sub - 1):
            load = load + lrx[step, o]
        answer = lax.dot_general(
            load, kinv_ref[...], NT, precision=HIGH, preferred_element_type=jnp.float32
        ).astype(jnp.bfloat16)
        wide = answer.astype(jnp.float32)
        for s in range(subs):
            spread = lax.dot_general(
                wide, table_ref[s], NT, preferred_element_type=jnp.float32
            ).astype(jnp.bfloat16)
            outs[s] = outs[s] + jnp.dot(
                spread, block_corner_ref[s], preferred_element_type=jnp.float32
            )
        energy = exchange(2 * step + 1, jnp.concatenate(outs, axis=1), D)
        for copy in sent:
            copy.wait_send()
        alpha = fit_next / energy
        L[...] = L[...] + alpha * D[:, :half]
        R[...] = R[...] - alpha * V[...]
        return fit_next

    lax.fori_loop(0, ITERS, body, jnp.ones((8, 1), jnp.float32))
    build(OHT, QO)
    gather(split(L[...]), QO, OHT, put(lam_out, 0), 3)
    gather(split(R[:, :half]), QO, OHT, put(res_out, 0), 3)


def per_device(
    right_side, dual_ops, precond_ops, corner_ops, coarse_inverse, sub_index, corner_map
):
    cases, lam = right_side.shape
    subs, br, order = dual_ops.shape
    kr, ncg = coarse_inverse.shape
    n_sub = lax.axis_size("sub")
    mine = lax.axis_index("coarse")
    slots = sub_index.reshape(subs, 4, br).transpose(1, 0, 2).reshape(2, 1, lam)
    pad = -ncg % LANES
    part = jnp.pad(coarse_inverse, ((0, 0), (0, pad)))
    table = (corner_map[:, :, None] == jnp.arange(ncg + pad)[None, None, :]).astype(jnp.float32)
    block_corner = lax.dynamic_slice_in_dim(corner_ops, mine * br, br, 2)
    bw = subs * br
    vmem = pl.BlockSpec(memory_space=pltpu.VMEM)
    hbm = pl.BlockSpec(memory_space=pl.ANY)
    f32 = lambda *dims: pltpu.VMEM(dims, jnp.float32)
    i32 = lambda *dims: pltpu.VMEM(dims, jnp.int32)
    b16 = lambda *dims: pltpu.VMEM(dims, jnp.bfloat16)
    dma = pltpu.SemaphoreType.DMA
    out = jax.ShapeDtypeStruct((cases, lam), jnp.float32)
    return pl.pallas_call(
        functools.partial(iterate_kernel, n_sub),
        out_shape=[out, out],
        in_specs=[vmem, hbm, hbm] + [vmem] * 6,
        out_specs=[vmem] * 2,
        scratch_shapes=[
            b16(subs, br, order), b16(subs, br, order),
            f32(8, 2 * lam), f32(8, 2 * lam), f32(8, lam), f32(8, 2 * lam), f32(8, lam),
            i32(1, lam), i32(1, lam), f32(4, kr, ncg + pad), f32(ncg + pad, ncg + pad),
            i32(8, lam), i32(8, lam), i32(8, lam),
            b16(WIDE, lam), b16(WIDE, lam), b16(WIDE, lam),
            b16(2 * ITERS, 8, bw // WIDE * 8, WIDE),
            f32(2 * ITERS, 8, LANES), f32(2 * ITERS, n_sub - 1, 8, LANES),
            f32(ITERS, 8, ncg + pad), f32(ITERS, n_sub - 1, 8, ncg + pad),
            dma((2,)), dma((6,)), dma((6,)),
            dma((7,)), dma((2 * ITERS, 7)),
            dma((n_sub - 1,)), dma((2 * ITERS,)),
            dma((n_sub - 1,)), dma((ITERS,)),
        ],
        compiler_params=pltpu.CompilerParams(
            collective_id=0, has_side_effects=True, vmem_limit_bytes=48 * 2**20
        ),
        name="iterate",
    )(
        right_side, dual_ops, precond_ops, corner_ops, block_corner, table,
        part, slots[0], slots[1],
    )


def solution(mesh):
    placed = (
        P(None, "sub"),
        P("sub", "coarse", None),
        P("sub", "coarse", None),
        P("sub", None, None),
        P("coarse", None),
        P("sub", None),
        P("sub", None),
    )
    return jax.shard_map(
        per_device,
        mesh=mesh,
        in_specs=placed,
        out_specs=(P(None, "sub"), P(None, "sub")),
        check_vma=False,
    )
```

```python
import functools

import jax
import jax.numpy as jnp
from jax import lax
from jax.experimental import pallas as pl
from jax.experimental.pallas import tpu as pltpu
from jax.sharding import PartitionSpec as P

ITERS = 4
LANES = 128
WIDE = 256
SHIFT = 8
CHUNK = 512
HIGH = lax.Precision.HIGHEST
MESH = pl.DeviceIdType.MESH
NT = (((1,), (1,)), ((), ()))


def iterate_kernel(
    n_sub, rhs_hbm, dual_hbm, precond_hbm, corner_hbm, inverse_hbm, index_hbm, map_hbm,
    lam_out, res_out,
    rhs_ref, corner_ref, part_ref, index_ref, map_ref, first_ref, second_ref, CT, CB, load_ref,
    dual_ref, precond_ref, D, R, L, V, prev_ref, first_prev, second_next, parts_ref, kinv_ref,
    Q1, Q2, QO, OH1, OH2, OHT,
    rx, dtx, drx, ltx, lrx, msem, psem, qsem, ssem, rsem, dssem, drsem, lssem, lrsem,
):
    j = lax.axis_index("sub")
    c = lax.axis_index("coarse")
    subs, br, order = dual_ref.shape
    bw = subs * br
    half = 2 * bw
    brows = bw // WIDE * 8
    kr = part_ref.shape[0]
    right = lax.rem(j + 1, n_sub)
    left = lax.rem(j + n_sub - 1, n_sub)
    high = c // 2
    halo = lax.rem(j + 1 - 2 * high + n_sub, n_sub)
    halo_slot = 6 + c - 4 * high
    peers = [(j, lax.rem(c + o, 4)) for o in range(1, 4)]

    smalls = [
        (index_hbm, index_ref), (rhs_hbm, rhs_ref), (inverse_hbm, part_ref),
        (map_hbm, map_ref), (corner_hbm, corner_ref),
    ]
    smalls = [
        pltpu.make_async_copy(a, b, msem.at[2 + i]) for i, (a, b) in enumerate(smalls)
    ]
    for copy in smalls:
        copy.start()
    loads = [
        pltpu.make_async_copy(precond_hbm, precond_ref, msem.at[0]),
        pltpu.make_async_copy(dual_hbm, dual_ref, msem.at[1]),
    ]
    for copy in loads:
        copy.start()

    barrier = pltpu.get_barrier_semaphore()
    friends = list(peers)
    for o in range(4):
        friends += [(left, o), (right, o)]
    for o in range(2, n_sub - 1):
        friends.append((lax.rem(j + o, n_sub), c))
    for f in friends:
        pl.semaphore_signal(barrier, inc=1, device_id=f, device_id_type=MESH)
    for copy in smalls:
        copy.wait()
    for b in range(4):
        ref = first_ref if b < 2 else second_ref
        for s in range(subs):
            at = (b % 2) * bw + s * br
            ref[:, at : at + br] = index_ref[s : s + 1, b * br : (b + 1) * br]
    pl.semaphore_wait(barrier, len(friends))

    setup = []
    plan = [
        (first_ref, first_prev, (right, c)),
        (second_ref, second_next, (left, c)),
        (rhs_ref, prev_ref, (right, c)),
    ] + [(part_ref, parts_ref.at[o], peers[o]) for o in range(3)]
    for i, (source, target, device) in enumerate(plan):
        copy = pltpu.make_async_remote_copy(
            src_ref=source, dst_ref=target, send_sem=psem.at[i], recv_sem=qsem.at[i],
            device_id=device, device_id_type=MESH,
        )
        copy.start()
        setup.append(copy)

    step_w = CHUNK
    chunks = half // step_w

    def chunk_at(o):
        return pl.ds(pl.multiple_of(o * step_w, step_w), step_w)

    def build(oh_ref, idx_ref):
        def body(o, carry):
            low = jnp.bitwise_and(idx_ref[:1, chunk_at(o)], WIDE - 1)
            rows = lax.broadcasted_iota(jnp.int32, (WIDE, step_w), 0)
            oh_ref[:, chunk_at(o)] = jnp.where(rows == low, 1.0, 0.0).astype(jnp.bfloat16)
            return carry

        lax.fori_loop(0, chunks, body, 0)

    def gather(src, idx_ref, oh_ref, finish, parts=1):
        count = src.shape[0] // 8 // parts

        def body(o, carry):
            hi = jnp.right_shift(idx_ref[:, chunk_at(o)], SHIFT)
            hi = jnp.broadcast_to(hi, (8, step_w))
            got = jnp.dot(src, oh_ref[:, chunk_at(o)], preferred_element_type=jnp.float32)
            acc = jnp.zeros((8, step_w), jnp.float32)
            for h in range(count):
                val = got[h * 8 : h * 8 + 8]
                for p in range(1, parts):
                    at = (p * count + h) * 8
                    val = val + got[at : at + 8]
                acc = jnp.where(hi == h, val, acc)
            finish(o, acc)
            return carry

        lax.fori_loop(0, chunks, body, 0)

    def put(ref, base):
        def finish(o, acc):
            ref[:, pl.ds(pl.multiple_of(base + o * step_w, step_w), step_w)] = acc

        return finish

    def put_index(ref):
        def finish(o, acc):
            pos = (acc[0:1] * WIDE + acc[1:2]).astype(jnp.int32)
            ref[:, chunk_at(o)] = jnp.broadcast_to(pos, (8, step_w))

        return finish

    def to_rows(x):
        return jnp.concatenate(
            [x[:, i * WIDE : (i + 1) * WIDE] for i in range(x.shape[1] // WIDE)], axis=0
        )

    def split(x):
        x = to_rows(x)
        a = x.astype(jnp.bfloat16)
        x = x - a.astype(jnp.float32)
        b = x.astype(jnp.bfloat16)
        x = x - b.astype(jnp.float32)
        return jnp.concatenate([a, b, x.astype(jnp.bfloat16)], axis=0)

    def inverse(idx_ref, shift, base, total):
        nh = half // WIDE
        acc = jnp.zeros((nh * 8, WIDE), jnp.float32)
        for o in range(chunks):
            rel = idx_ref[:, o * step_w : (o + 1) * step_w] + shift
            rel = jnp.where(rel < 0, rel + total, rel)
            hi = jnp.right_shift(rel, SHIFT)
            low = jnp.bitwise_and(rel, WIDE - 1)
            pos = lax.broadcasted_iota(jnp.int32, (nh * 8, step_w), 1) + (base + o * step_w)
            row = lax.broadcasted_iota(jnp.int32, (nh * 8, step_w), 0)
            digit = jnp.bitwise_and(row, 7)
            val = jnp.where(digit == 0, jnp.right_shift(pos, SHIFT), jnp.bitwise_and(pos, WIDE - 1))
            keep = jnp.logical_and(jnp.right_shift(row, 3) == hi, digit < 2)
            left_side = jnp.where(keep, val, 0).astype(jnp.float32).astype(jnp.bfloat16)
            rows = lax.broadcasted_iota(jnp.int32, (WIDE, step_w), 0)
            right_side = jnp.where(rows == low, 1.0, 0.0).astype(jnp.bfloat16)
            acc = acc + lax.dot_general(
                left_side, right_side, NT, preferred_element_type=jnp.float32
            )
        return acc

    total = n_sub * half
    pf_own = inverse(first_ref, -j * half, 0, total)
    ps = inverse(second_ref, -j * half, 0, total)
    for h in range(half // WIDE):
        pos = (pf_own[h * 8 : h * 8 + 1] * WIDE + pf_own[h * 8 + 1 : h * 8 + 2]).astype(jnp.int32)
        QO[:, h * WIDE : (h + 1) * WIDE] = jnp.broadcast_to(pos, (8, WIDE))
    Q1[...] = jnp.broadcast_to(first_ref[...] - j * half, (8, half))
    rel = second_ref[...] - j * half
    rel = jnp.where(rel < 0, rel + total, rel)
    rel = jnp.where(rel < half, rel, rel - (total - 2 * half))
    Q2[...] = jnp.broadcast_to(rel, (8, half))
    build(OH1, Q1)
    build(OH2, Q2)
    D[...] = jnp.zeros_like(D)
    L[...] = jnp.zeros_like(L)
    kinv_ref[...] = jnp.zeros_like(kinv_ref)
    load_ref[...] = jnp.zeros_like(load_ref)
    for s in range(subs):
        rows = lax.broadcasted_iota(jnp.int32, (CT.shape[1], map_ref.shape[1]), 0)
        table = jnp.where(rows == map_ref[s : s + 1, :], 1.0, 0.0).astype(jnp.bfloat16)
        CT[s] = jnp.dot(
            table, corner_ref[s], preferred_element_type=jnp.float32
        ).astype(jnp.bfloat16)
        at = pl.ds(pl.multiple_of(c * br, br), br)
        CB[:, s * br : (s + 1) * br] = CT[s, :, at]
    parts_ref[3] = part_ref[...]
    own_rows = split(rhs_ref[...])
    gather(own_rows, Q1, OH1, put(R, 0), 3)
    for copy in setup:
        copy.wait_recv()
    for b in range(4):
        kinv_ref[b * kr : (b + 1) * kr, : part_ref.shape[1]] = parts_ref[lax.rem(c + 7 - b, 4)]
    prev_rows = split(prev_ref[...])
    n = half // WIDE * 8
    both = []
    for p in range(3):
        both += [own_rows[p * n : (p + 1) * n], prev_rows[p * n : (p + 1) * n]]
    gather(jnp.concatenate(both, axis=0), Q2, OH2, put(R, half), 3)
    ps = ps + inverse(second_next, -j * half, half, total)
    pf_prev = inverse(first_prev, -left * half, half, total)
    gather(ps.astype(jnp.bfloat16), Q1, OH1, put_index(Q1))
    pf = jnp.concatenate([pf_own, pf_prev], axis=0).astype(jnp.bfloat16)
    gather(pf, Q2, OH2, put_index(Q2))
    build(OH1, Q1)
    build(OH2, Q2)
    for copy in setup:
        copy.wait_send()

    def gathered(ref, s):
        parts = []
        for b in range(4):
            part = ref[:, b * bw + s * br : b * bw + (s + 1) * br]
            parts.append(part if b < 2 else -part)
        return jnp.concatenate(parts, axis=1).astype(jnp.bfloat16)

    def unpack(block):
        wide = block.astype(jnp.float32)
        return jnp.concatenate([wide[i * 8 : i * 8 + 8] for i in range(brows // 8)], axis=1)

    def exchange(app, terms, vec_ref):
        rx[app, 0] = to_rows(terms).astype(jnp.bfloat16)
        copies = []
        for i in range(7):
            if i < 4:
                slot, device = halo_slot, (halo, i)
            else:
                slot, device = i - 3, peers[i - 4]
            copy = pltpu.make_async_remote_copy(
                src_ref=rx.at[app, 0], dst_ref=rx.at[app, slot],
                send_sem=ssem.at[i], recv_sem=rsem.at[app, slot - 1],
                device_id=device, device_id_type=MESH,
            )
            copy.start()
            copies.append(copy)
        for slot in range(1, 4):
            pltpu.make_async_copy(
                rx.at[app, slot], rx.at[app, slot], rsem.at[app, slot - 1]
            ).wait()
        packed = [rx[app, lax.rem(c + 4 - b, 4)] for b in range(4)]
        blocks = [unpack(p) for p in packed]
        part = jnp.zeros((8, LANES), jnp.float32)
        for b in range(4):
            prod = vec_ref[:, b * bw : (b + 1) * bw] * blocks[b]
            for k in range(bw // LANES):
                piece = prod[:, k * LANES : (k + 1) * LANES]
                part = part + piece if b < 2 else part - piece
        dtx[app] = part
        dots = []
        for o in range(1, n_sub):
            copy = pltpu.make_async_remote_copy(
                src_ref=dtx.at[app], dst_ref=drx.at[app, o - 1],
                send_sem=dssem.at[o - 1], recv_sem=drsem.at[app],
                device_id=(lax.rem(j + o, n_sub), c), device_id_type=MESH,
            )
            copy.start()
            dots.append(copy)
        for b in range(4):
            V[:, b * bw : (b + 1) * bw] = blocks[b]
        for slot in range(4, 8):
            pltpu.make_async_copy(
                rx.at[app, slot], rx.at[app, slot], rsem.at[app, slot - 1]
            ).wait()

        def less(o, acc):
            V[:, chunk_at(o)] = V[:, chunk_at(o)] - acc

        def more(o, acc):
            at = pl.ds(pl.multiple_of(half + o * step_w, step_w), step_w)
            V[:, at] = acc - V[:, at]

        gather(
            jnp.concatenate([packed[2], packed[3], rx[app, 4], rx[app, 5]], axis=0),
            Q1, OH1, less,
        )
        gather(
            jnp.concatenate([packed[0], packed[1], rx[app, 6], rx[app, 7]], axis=0),
            Q2, OH2, more,
        )
        return part, copies, dots

    def finish_dot(app, part, copies, dots):
        pltpu.make_async_copy(drx.at[app], drx.at[app], drsem.at[app]).wait()
        total = part
        for o in range(n_sub - 1):
            total = total + drx[app, o]
        for copy in copies + dots:
            copy.wait_send()
        return jnp.sum(total, axis=1, keepdims=True)

    def product(ops_ref, vecs):
        return [
            lax.dot_general(vecs[s], ops_ref[s], NT, preferred_element_type=jnp.float32)
            for s in range(subs)
        ]

    for copy in loads:
        copy.wait()

    def body(step, fit):
        vecs = [gathered(R, s) for s in range(subs)]
        terms = jnp.concatenate(product(precond_ref, vecs), axis=1)
        pending = exchange(2 * step, terms, R)

        load = jnp.zeros((8, kinv_ref.shape[0]), jnp.float32)
        for s in range(subs):
            load = load + lax.dot_general(
                gathered(V, s), CT[s], NT, preferred_element_type=jnp.float32
            )
        ltx[step] = load
        sent = []
        for o in range(1, n_sub):
            copy = pltpu.make_async_remote_copy(
                src_ref=ltx.at[step], dst_ref=lrx.at[step, o - 1],
                send_sem=lssem.at[o - 1], recv_sem=lrsem.at[step],
                device_id=(lax.rem(j + o, n_sub), c), device_id_type=MESH,
            )
            copy.start()
            sent.append(copy)
        fit_next = finish_dot(2 * step, *pending)
        beta = fit_next / fit
        D[...] = V[...] + beta * D[...]

        vecs = [gathered(D, s) for s in range(subs)]
        terms = jnp.concatenate(product(dual_ref, vecs), axis=1)
        pltpu.make_async_copy(lrx.at[step], lrx.at[step], lrsem.at[step]).wait()
        for o in range(n_sub - 1):
            load = load + lrx[step, o]
        load = load + beta * load_ref[...]
        load_ref[...] = load
        answer = lax.dot_general(
            load, kinv_ref[...], NT, precision=HIGH, preferred_element_type=jnp.float32
        ).astype(jnp.bfloat16)
        terms = terms + jnp.dot(answer, CB[...], preferred_element_type=jnp.float32)
        energy = finish_dot(2 * step + 1, *exchange(2 * step + 1, terms, D))
        for copy in sent:
            copy.wait_send()
        alpha = fit_next / energy
        L[...] = L[...] + alpha * D[:, :half]
        R[...] = R[...] - alpha * V[...]
        return fit_next

    lax.fori_loop(0, ITERS, body, jnp.ones((8, 1), jnp.float32))
    build(OHT, QO)
    gather(split(L[...]), QO, OHT, put(lam_out, 0), 3)
    gather(split(R[:, :half]), QO, OHT, put(res_out, 0), 3)


def per_device(
    right_side, dual_ops, precond_ops, corner_ops, coarse_inverse, sub_index, corner_map
):
    cases, lam = right_side.shape
    subs, br, order = dual_ops.shape
    kr, ncg = coarse_inverse.shape
    n_sub = lax.axis_size("sub")
    pad = -ncg % LANES
    nc = corner_map.shape[1]
    bw = subs * br
    vmem = pl.BlockSpec(memory_space=pltpu.VMEM)
    hbm = pl.BlockSpec(memory_space=pl.ANY)
    f32 = lambda *dims: pltpu.VMEM(dims, jnp.float32)
    i32 = lambda *dims: pltpu.VMEM(dims, jnp.int32)
    b16 = lambda *dims: pltpu.VMEM(dims, jnp.bfloat16)
    dma = pltpu.SemaphoreType.DMA
    out = jax.ShapeDtypeStruct((cases, lam), jnp.float32)
    return pl.pallas_call(
        functools.partial(iterate_kernel, n_sub),
        out_shape=[out, out],
        in_specs=[hbm] * 7,
        out_specs=[vmem] * 2,
        scratch_shapes=[
            f32(8, lam), b16(subs, nc, order), f32(kr, ncg), i32(subs, order), i32(subs, nc),
            i32(1, lam), i32(1, lam), b16(subs, ncg + pad, order), b16(ncg + pad, bw),
            f32(8, ncg + pad),
            b16(subs, br, order), b16(subs, br, order),
            f32(8, 2 * lam), f32(8, 2 * lam), f32(8, lam), f32(8, 2 * lam), f32(8, lam),
            i32(1, lam), i32(1, lam), f32(4, kr, ncg), f32(ncg + pad, ncg + pad),
            i32(8, lam), i32(8, lam), i32(8, lam),
            b16(WIDE, lam), b16(WIDE, lam), b16(WIDE, lam),
            b16(2 * ITERS, 8, bw // WIDE * 8, WIDE),
            f32(2 * ITERS, 8, LANES), f32(2 * ITERS, n_sub - 1, 8, LANES),
            f32(ITERS, 8, ncg + pad), f32(ITERS, n_sub - 1, 8, ncg + pad),
            dma((7,)), dma((6,)), dma((6,)),
            dma((7,)), dma((2 * ITERS, 7)),
            dma((n_sub - 1,)), dma((2 * ITERS,)),
            dma((n_sub - 1,)), dma((ITERS,)),
        ],
        compiler_params=pltpu.CompilerParams(
            collective_id=0, has_side_effects=True, vmem_limit_bytes=48 * 2**20
        ),
        name="iterate",
    )(
        right_side, dual_ops, precond_ops, corner_ops, coarse_inverse, sub_index, corner_map,
    )


def solution(mesh):
    placed = (
        P(None, "sub"),
        P("sub", "coarse", None),
        P("sub", "coarse", None),
        P("sub", None, None),
        P("coarse", None),
        P("sub", None),
        P("sub", None),
    )
    return jax.shard_map(
        per_device,
        mesh=mesh,
        in_specs=placed,
        out_specs=(P(None, "sub"), P(None, "sub")),
        check_vma=False,
    )
```

```python
import functools

import jax
import jax.numpy as jnp
from jax import lax
from jax.experimental import pallas as pl
from jax.experimental.pallas import tpu as pltpu
from jax.sharding import PartitionSpec as P

ITERS = 4
LANES = 128
WIDE = 256
SHIFT = 8
CHUNK = 512
HIGH = lax.Precision.HIGHEST
MESH = pl.DeviceIdType.MESH
NT = (((1,), (1,)), ((), ()))


def iterate_kernel(
    n_sub, rhs_hbm, dual_hbm, precond_hbm, corner_hbm, inverse_hbm, index_hbm, map_hbm,
    lam_out, res_out,
    rhs_ref, corner_ref, part_ref, index_ref, map_ref, first_ref, second_ref, CT, CB, load_ref,
    dual_ref, precond_ref, D, R, L, V, prev_ref, first_prev, second_next, parts_ref, kinv_ref,
    Q1, Q2, QO, OH1, OH2, OHT,
    rx, dtx, drx, ltx, lrx, msem, psem, qsem, ssem, rsem, dssem, drsem, lssem, lrsem,
):
    j = lax.axis_index("sub")
    c = lax.axis_index("coarse")
    subs, br, order = dual_ref.shape
    bw = subs * br
    half = 2 * bw
    brows = bw // WIDE * 8
    kr = part_ref.shape[0]
    right = lax.rem(j + 1, n_sub)
    left = lax.rem(j + n_sub - 1, n_sub)
    high = c // 2
    halo = lax.rem(j + 1 - 2 * high + n_sub, n_sub)
    halo_slot = 6 + c - 4 * high
    peers = [(j, lax.rem(c + o, 4)) for o in range(1, 4)]

    smalls = [
        (index_hbm, index_ref), (rhs_hbm, rhs_ref), (inverse_hbm, part_ref),
        (map_hbm, map_ref), (corner_hbm, corner_ref),
    ]
    smalls = [
        pltpu.make_async_copy(a, b, msem.at[2 + i]) for i, (a, b) in enumerate(smalls)
    ]
    for copy in smalls:
        copy.start()
    loads = [
        pltpu.make_async_copy(precond_hbm, precond_ref, msem.at[0]),
        pltpu.make_async_copy(dual_hbm, dual_ref, msem.at[1]),
    ]
    for copy in loads:
        copy.start()

    barrier = pltpu.get_barrier_semaphore()
    friends = list(peers)
    for o in range(4):
        friends += [(left, o), (right, o)]
    for o in range(2, n_sub - 1):
        friends.append((lax.rem(j + o, n_sub), c))
    for f in friends:
        pl.semaphore_signal(barrier, inc=1, device_id=f, device_id_type=MESH)
    for copy in smalls:
        copy.wait()
    for b in range(4):
        ref = first_ref if b < 2 else second_ref
        for s in range(subs):
            at = (b % 2) * bw + s * br
            ref[:, at : at + br] = index_ref[s : s + 1, b * br : (b + 1) * br]
    pl.semaphore_wait(barrier, len(friends))

    setup = []
    plan = [
        (first_ref, first_prev, (right, c)),
        (second_ref, second_next, (left, c)),
        (rhs_ref, prev_ref, (right, c)),
    ] + [(part_ref, parts_ref.at[o], peers[o]) for o in range(3)]
    for i, (source, target, device) in enumerate(plan):
        copy = pltpu.make_async_remote_copy(
            src_ref=source, dst_ref=target, send_sem=psem.at[i], recv_sem=qsem.at[i],
            device_id=device, device_id_type=MESH,
        )
        copy.start()
        setup.append(copy)

    step_w = CHUNK
    chunks = half // step_w

    def chunk_at(o):
        return pl.ds(pl.multiple_of(o * step_w, step_w), step_w)

    def build(oh_ref, idx_ref):
        def body(o, carry):
            low = jnp.bitwise_and(idx_ref[:1, chunk_at(o)], WIDE - 1)
            rows = lax.broadcasted_iota(jnp.int32, (WIDE, step_w), 0)
            oh_ref[:, chunk_at(o)] = jnp.where(rows == low, 1.0, 0.0).astype(jnp.bfloat16)
            return carry

        lax.fori_loop(0, chunks, body, 0)

    def gather(src, idx_ref, oh_ref, finish, parts=1):
        count = src.shape[0] // 8 // parts

        def body(o, carry):
            hi = jnp.right_shift(idx_ref[:, chunk_at(o)], SHIFT)
            hi = jnp.broadcast_to(hi, (8, step_w))
            got = jnp.dot(src, oh_ref[:, chunk_at(o)], preferred_element_type=jnp.float32)
            acc = jnp.zeros((8, step_w), jnp.float32)
            for h in range(count):
                val = got[h * 8 : h * 8 + 8]
                for p in range(1, parts):
                    at = (p * count + h) * 8
                    val = val + got[at : at + 8]
                acc = jnp.where(hi == h, val, acc)
            finish(o, acc)
            return carry

        lax.fori_loop(0, chunks, body, 0, unroll=True)

    def put(ref, base):
        def finish(o, acc):
            ref[:, pl.ds(pl.multiple_of(base + o * step_w, step_w), step_w)] = acc

        return finish

    def put_index(ref):
        def finish(o, acc):
            pos = (acc[0:1] * WIDE + acc[1:2]).astype(jnp.int32)
            ref[:, chunk_at(o)] = jnp.broadcast_to(pos, (8, step_w))

        return finish

    def to_rows(x):
        return jnp.concatenate(
            [x[:, i * WIDE : (i + 1) * WIDE] for i in range(x.shape[1] // WIDE)], axis=0
        )

    def split(x):
        x = to_rows(x)
        a = x.astype(jnp.bfloat16)
        x = x - a.astype(jnp.float32)
        b = x.astype(jnp.bfloat16)
        x = x - b.astype(jnp.float32)
        return jnp.concatenate([a, b, x.astype(jnp.bfloat16)], axis=0)

    def inverse(idx_ref, shift, base, total):
        nh = half // WIDE
        acc = jnp.zeros((nh * 8, WIDE), jnp.float32)
        for o in range(chunks):
            rel = idx_ref[:, o * step_w : (o + 1) * step_w] + shift
            rel = jnp.where(rel < 0, rel + total, rel)
            hi = jnp.right_shift(rel, SHIFT)
            low = jnp.bitwise_and(rel, WIDE - 1)
            pos = lax.broadcasted_iota(jnp.int32, (nh * 8, step_w), 1) + (base + o * step_w)
            row = lax.broadcasted_iota(jnp.int32, (nh * 8, step_w), 0)
            digit = jnp.bitwise_and(row, 7)
            val = jnp.where(digit == 0, jnp.right_shift(pos, SHIFT), jnp.bitwise_and(pos, WIDE - 1))
            keep = jnp.logical_and(jnp.right_shift(row, 3) == hi, digit < 2)
            left_side = jnp.where(keep, val, 0).astype(jnp.float32).astype(jnp.bfloat16)
            rows = lax.broadcasted_iota(jnp.int32, (WIDE, step_w), 0)
            right_side = jnp.where(rows == low, 1.0, 0.0).astype(jnp.bfloat16)
            acc = acc + lax.dot_general(
                left_side, right_side, NT, preferred_element_type=jnp.float32
            )
        return acc

    total = n_sub * half
    pf_own = inverse(first_ref, -j * half, 0, total)
    ps = inverse(second_ref, -j * half, 0, total)
    for h in range(half // WIDE):
        pos = (pf_own[h * 8 : h * 8 + 1] * WIDE + pf_own[h * 8 + 1 : h * 8 + 2]).astype(jnp.int32)
        QO[:, h * WIDE : (h + 1) * WIDE] = jnp.broadcast_to(pos, (8, WIDE))
    Q1[...] = jnp.broadcast_to(first_ref[...] - j * half, (8, half))
    rel = second_ref[...] - j * half
    rel = jnp.where(rel < 0, rel + total, rel)
    rel = jnp.where(rel < half, rel, rel - (total - 2 * half))
    Q2[...] = jnp.broadcast_to(rel, (8, half))
    build(OH1, Q1)
    build(OH2, Q2)
    D[...] = jnp.zeros_like(D)
    L[...] = jnp.zeros_like(L)
    kinv_ref[...] = jnp.zeros_like(kinv_ref)
    load_ref[...] = jnp.zeros_like(load_ref)
    for s in range(subs):
        rows = lax.broadcasted_iota(jnp.int32, (CT.shape[1], map_ref.shape[1]), 0)
        table = jnp.where(rows == map_ref[s : s + 1, :], 1.0, 0.0).astype(jnp.bfloat16)
        CT[s] = jnp.dot(
            table, corner_ref[s], preferred_element_type=jnp.float32
        ).astype(jnp.bfloat16)
        at = pl.ds(pl.multiple_of(c * br, br), br)
        CB[:, s * br : (s + 1) * br] = CT[s, :, at]
    parts_ref[3] = part_ref[...]
    own_rows = split(rhs_ref[...])
    gather(own_rows, Q1, OH1, put(R, 0), 3)
    for copy in setup:
        copy.wait_recv()
    for b in range(4):
        kinv_ref[b * kr : (b + 1) * kr, : part_ref.shape[1]] = parts_ref[lax.rem(c + 7 - b, 4)]
    prev_rows = split(prev_ref[...])
    n = half // WIDE * 8
    both = []
    for p in range(3):
        both += [own_rows[p * n : (p + 1) * n], prev_rows[p * n : (p + 1) * n]]
    gather(jnp.concatenate(both, axis=0), Q2, OH2, put(R, half), 3)
    ps = ps + inverse(second_next, -j * half, half, total)
    pf_prev = inverse(first_prev, -left * half, half, total)
    gather(ps.astype(jnp.bfloat16), Q1, OH1, put_index(Q1))
    pf = jnp.concatenate([pf_own, pf_prev], axis=0).astype(jnp.bfloat16)
    gather(pf, Q2, OH2, put_index(Q2))
    build(OH1, Q1)
    build(OH2, Q2)
    for copy in setup:
        copy.wait_send()

    def gathered(ref, s):
        parts = []
        for b in range(4):
            part = ref[:, b * bw + s * br : b * bw + (s + 1) * br]
            parts.append(part if b < 2 else -part)
        return jnp.concatenate(parts, axis=1).astype(jnp.bfloat16)

    def unpack(block):
        wide = block.astype(jnp.float32)
        return jnp.concatenate([wide[i * 8 : i * 8 + 8] for i in range(brows // 8)], axis=1)

    def exchange(app, terms, vec_ref):
        rx[app, 0] = to_rows(terms).astype(jnp.bfloat16)
        copies = []
        for i in range(7):
            if i < 4:
                slot, device = halo_slot, (halo, i)
            else:
                slot, device = i - 3, peers[i - 4]
            copy = pltpu.make_async_remote_copy(
                src_ref=rx.at[app, 0], dst_ref=rx.at[app, slot],
                send_sem=ssem.at[i], recv_sem=rsem.at[app, slot - 1],
                device_id=device, device_id_type=MESH,
            )
            copy.start()
            copies.append(copy)
        for slot in range(1, 4):
            pltpu.make_async_copy(
                rx.at[app, slot], rx.at[app, slot], rsem.at[app, slot - 1]
            ).wait()
        packed = [rx[app, lax.rem(c + 4 - b, 4)] for b in range(4)]
        blocks = [unpack(p) for p in packed]
        part = jnp.zeros((8, LANES), jnp.float32)
        for b in range(4):
            prod = vec_ref[:, b * bw : (b + 1) * bw] * blocks[b]
            for k in range(bw // LANES):
                piece = prod[:, k * LANES : (k + 1) * LANES]
                part = part + piece if b < 2 else part - piece
        dtx[app] = part
        dots = []
        for o in range(1, n_sub):
            copy = pltpu.make_async_remote_copy(
                src_ref=dtx.at[app], dst_ref=drx.at[app, o - 1],
                send_sem=dssem.at[o - 1], recv_sem=drsem.at[app],
                device_id=(lax.rem(j + o, n_sub), c), device_id_type=MESH,
            )
            copy.start()
            dots.append(copy)
        for b in range(4):
            V[:, b * bw : (b + 1) * bw] = blocks[b]
        for slot in range(4, 8):
            pltpu.make_async_copy(
                rx.at[app, slot], rx.at[app, slot], rsem.at[app, slot - 1]
            ).wait()

        def less(o, acc):
            V[:, chunk_at(o)] = V[:, chunk_at(o)] - acc

        def more(o, acc):
            at = pl.ds(pl.multiple_of(half + o * step_w, step_w), step_w)
            V[:, at] = acc - V[:, at]

        gather(
            jnp.concatenate([packed[2], packed[3], rx[app, 4], rx[app, 5]], axis=0),
            Q1, OH1, less,
        )
        gather(
            jnp.concatenate([packed[0], packed[1], rx[app, 6], rx[app, 7]], axis=0),
            Q2, OH2, more,
        )
        return part, copies, dots

    def finish_dot(app, part, copies, dots):
        pltpu.make_async_copy(drx.at[app], drx.at[app], drsem.at[app]).wait()
        total = part
        for o in range(n_sub - 1):
            total = total + drx[app, o]
        for copy in copies + dots:
            copy.wait_send()
        return jnp.sum(total, axis=1, keepdims=True)

    def product(ops_ref, vecs):
        return [
            lax.dot_general(vecs[s], ops_ref[s], NT, preferred_element_type=jnp.float32)
            for s in range(subs)
        ]

    for copy in loads:
        copy.wait()

    def body(step, fit):
        vecs = [gathered(R, s) for s in range(subs)]
        terms = jnp.concatenate(product(precond_ref, vecs), axis=1)
        pending = exchange(2 * step, terms, R)

        load = jnp.zeros((8, kinv_ref.shape[0]), jnp.float32)
        for s in range(subs):
            load = load + lax.dot_general(
                gathered(V, s), CT[s], NT, preferred_element_type=jnp.float32
            )
        ltx[step] = load
        sent = []
        for o in range(1, n_sub):
            copy = pltpu.make_async_remote_copy(
                src_ref=ltx.at[step], dst_ref=lrx.at[step, o - 1],
                send_sem=lssem.at[o - 1], recv_sem=lrsem.at[step],
                device_id=(lax.rem(j + o, n_sub), c), device_id_type=MESH,
            )
            copy.start()
            sent.append(copy)
        fit_next = finish_dot(2 * step, *pending)
        beta = fit_next / fit
        D[...] = V[...] + beta * D[...]

        vecs = [gathered(D, s) for s in range(subs)]
        terms = jnp.concatenate(product(dual_ref, vecs), axis=1)
        pltpu.make_async_copy(lrx.at[step], lrx.at[step], lrsem.at[step]).wait()
        for o in range(n_sub - 1):
            load = load + lrx[step, o]
        load = load + beta * load_ref[...]
        load_ref[...] = load
        answer = lax.dot_general(
            load, kinv_ref[...], NT, precision=HIGH, preferred_element_type=jnp.float32
        ).astype(jnp.bfloat16)
        terms = terms + jnp.dot(answer, CB[...], preferred_element_type=jnp.float32)
        energy = finish_dot(2 * step + 1, *exchange(2 * step + 1, terms, D))
        for copy in sent:
            copy.wait_send()
        alpha = fit_next / energy
        L[...] = L[...] + alpha * D[:, :half]
        R[...] = R[...] - alpha * V[...]
        return fit_next

    lax.fori_loop(0, ITERS, body, jnp.ones((8, 1), jnp.float32))
    build(OHT, QO)
    gather(split(L[...]), QO, OHT, put(lam_out, 0), 3)
    gather(split(R[:, :half]), QO, OHT, put(res_out, 0), 3)


def per_device(
    right_side, dual_ops, precond_ops, corner_ops, coarse_inverse, sub_index, corner_map
):
    cases, lam = right_side.shape
    subs, br, order = dual_ops.shape
    kr, ncg = coarse_inverse.shape
    n_sub = lax.axis_size("sub")
    pad = -ncg % LANES
    nc = corner_map.shape[1]
    bw = subs * br
    vmem = pl.BlockSpec(memory_space=pltpu.VMEM)
    hbm = pl.BlockSpec(memory_space=pltpu.HBM)
    f32 = lambda *dims: pltpu.VMEM(dims, jnp.float32)
    i32 = lambda *dims: pltpu.VMEM(dims, jnp.int32)
    b16 = lambda *dims: pltpu.VMEM(dims, jnp.bfloat16)
    dma = pltpu.SemaphoreType.DMA
    out = jax.ShapeDtypeStruct((cases, lam), jnp.float32)
    return pl.pallas_call(
        functools.partial(iterate_kernel, n_sub),
        out_shape=[out, out],
        in_specs=[hbm] * 7,
        out_specs=[vmem] * 2,
        scratch_shapes=[
            f32(8, lam), b16(subs, nc, order), f32(kr, ncg), i32(subs, order), i32(subs, nc),
            i32(1, lam), i32(1, lam), b16(subs, ncg + pad, order), b16(ncg + pad, bw),
            f32(8, ncg + pad),
            b16(subs, br, order), b16(subs, br, order),
            f32(8, 2 * lam), f32(8, 2 * lam), f32(8, lam), f32(8, 2 * lam), f32(8, lam),
            i32(1, lam), i32(1, lam), f32(4, kr, ncg), f32(ncg + pad, ncg + pad),
            i32(8, lam), i32(8, lam), i32(8, lam),
            b16(WIDE, lam), b16(WIDE, lam), b16(WIDE, lam),
            b16(2 * ITERS, 8, bw // WIDE * 8, WIDE),
            f32(2 * ITERS, 8, LANES), f32(2 * ITERS, n_sub - 1, 8, LANES),
            f32(ITERS, 8, ncg + pad), f32(ITERS, n_sub - 1, 8, ncg + pad),
            dma((7,)), dma((6,)), dma((6,)),
            dma((7,)), dma((2 * ITERS, 7)),
            dma((n_sub - 1,)), dma((2 * ITERS,)),
            dma((n_sub - 1,)), dma((ITERS,)),
        ],
        compiler_params=pltpu.CompilerParams(
            collective_id=0, has_side_effects=True, vmem_limit_bytes=48 * 2**20
        ),
        name="iterate",
    )(
        right_side, dual_ops, precond_ops, corner_ops, coarse_inverse, sub_index, corner_map,
    )


def solution(mesh):
    placed = (
        P(None, "sub"),
        P("sub", "coarse", None),
        P("sub", "coarse", None),
        P("sub", None, None),
        P("coarse", None),
        P("sub", None),
        P("sub", None),
    )
    return jax.shard_map(
        per_device,
        mesh=mesh,
        in_specs=placed,
        out_specs=(P(None, "sub"), P(None, "sub")),
        check_vma=False,
    )
```
